256 devices in a mesh: seq: 32 (over y, z_hi, core), tp: 4 (over x), grp: 2 (over z_lo).
Axes of the slice: x: 4, y: 4, z: 8 (z_hi: 4, z_lo: 2; z = z_hi * 2 + z_lo), core: 2. Of those that a mesh axis runs over, the one named last changes fastest.
Arguments:
- queries: bfloat16 [2, 4096, 32, 128], P('grp', 'seq', 'tp'), may hold values from -96 to 96
- span_kv: bfloat16 [2, 4096, 4, 256], P('grp', 'seq', 'tp'), may hold values from -4 to 4
- prior_kv: bfloat16 [2, 131072, 4, 256], P('grp', 'seq', 'tp'), may hold values from -4 to 4
- list_ids: int32 [2, 32, 32], P('grp'), may hold values from 0 to 1023, as said below
- out_weight: bfloat16 [4096, 4096], P('tp'), may hold values from -0.25 to 0.25
- pool_kv: bfloat16 [2, 32, 16, 128, 4, 256], P('grp', 'seq', None, None, 'tp'), may hold values from -4 to 4
- page_table: int32 [2, 32, 16], P('grp', 'seq'), may hold values from 0 to 15, each once within a row
- cache_lens: int32 [2, 32], P('grp', 'seq'), may hold values from 1 to 2048, as said below
- hist_kv: bfloat16 [2, 32, 8, 128, 4, 256], P('grp', 'seq', None, None, 'tp'), may hold values from -4 to 4
- dec_q: bfloat16 [2, 2, 32, 8, 32, 128], P('grp', None, 'seq', None, 'tp'), may hold values from -96 to 96
- dec_kv: bfloat16 [2, 2, 32, 8, 4, 256], P('grp', None, 'seq', None, 'tp'), may hold values from -4 to 4
- parents: int32 [2, 32, 8], P('grp', 'seq'), may hold values from 0 to 7
- dest: int32 [2, 32], P('grp'), may hold values from 0 to 31, as said below
Outputs:
- prefill_out: bfloat16 [2, 4096, 4096], P('grp', 'seq', 'tp')
- decode_out: bfloat16 [2, 2, 32, 8, 32, 128], P('grp', None, 'seq', None, 'tp')
The draws below stay inside these ranges and needn't reach their ends.
Inputs may be any that keep to these rules, and one draw needn't show every extreme that they name: Each row of list_ids is strictly increasing; at most 2 ids of a row lie in one aligned run of 32 blocks, and every row has a run holding exactly 2. `dest`: no request receives more than 3 prompt blocks, and in each half one request receives exactly 2. `cache_lens`: in each half one request has exactly 2048. `page_table`: each row lists each page once.
All inputs are finite; a program needn't handle non-finite values.
Results may differ from the reference program's by a relative error of at most 0.015.
Values may be sent and summed in bfloat16 or wider, within the bound.
No kernel may reach another device: no remote copies, remote signals or barrier semaphores. Data moves between devices by JAX's collectives and lax.ppermute only.
A program may use at most 128 MiB of HBM per device.

```python
import jax
import jax.numpy as jnp
from jax import lax

DH = 128
HQ = 32
HK = 4
DOUT = 4096
SPAN_DEV = 128
BLK = 128
KVB_DEV = 32
BEAMS = 8
STEPS = 2
PAGES = 16
HIST = 128
HAND = 2
LIST = 32
PRIOR = 131072
CAP = 2048
N_SEQ = 32
N_GRP = 2


def span_base(key):
    key = jax.random.fold_in(key, 101)
    return jnp.clip(jax.random.normal(key, (N_GRP, N_SEQ * SPAN_DEV, HK, DH), jnp.float32), -4.0, 4.0)


def decode_base(key):
    key = jax.random.fold_in(key, 102)
    return jnp.clip(jax.random.normal(key, (N_GRP, STEPS, N_SEQ, BEAMS, HK, DH), jnp.float32), -4.0, 4.0)


def draw_span_kv(key, part):
    keys_part = span_base(key)
    key = jax.random.fold_in(key, 11)
    values = jnp.clip(jax.random.normal(key, keys_part.shape, jnp.float32), -4.0, 4.0)
    return jnp.concatenate([keys_part, values], axis=-1).astype(jnp.bfloat16)


def draw_queries(key, part):
    key = jax.random.fold_in(key, 12)
    shape = (N_GRP, N_SEQ * SPAN_DEV, HQ, DH)
    return jnp.clip(3.0 * jax.random.normal(key, shape, jnp.float32), -16.0, 16.0).astype(jnp.bfloat16)


def draw_dec_kv(key, part):
    keys_part = decode_base(key)
    key = jax.random.fold_in(key, 13)
    values = jnp.clip(jax.random.normal(key, keys_part.shape, jnp.float32), -4.0, 4.0)
    return jnp.concatenate([keys_part, values], axis=-1).astype(jnp.bfloat16)


def draw_dec_q(key, part):
    key = jax.random.fold_in(key, 14)
    shape = (N_GRP, STEPS, N_SEQ, BEAMS, HQ, DH)
    return jnp.clip(3.0 * jax.random.normal(key, shape, jnp.float32), -16.0, 16.0).astype(jnp.bfloat16)


def draw_list_ids(key, part):
    key = jax.random.fold_in(key, 21)

    def one_row(row_key):
        order_key, low_key, high_key, single_key = jax.random.split(row_key, 4)
        order = jax.random.permutation(order_key, N_SEQ)
        rank = jnp.arange(N_SEQ)
        by_rank = jnp.where(rank < N_SEQ // 4, 2, jnp.where(rank < 3 * N_SEQ // 4, 1, 0)).astype(jnp.int32)
        counts = jnp.zeros((N_SEQ,), jnp.int32).at[order].set(by_rank)
        start = jnp.cumsum(counts) - counts
        low = jax.random.randint(low_key, (N_SEQ,), 0, KVB_DEV // 2)
        high = KVB_DEV // 2 + jax.random.randint(high_key, (N_SEQ,), 0, KVB_DEV // 2)
        single = jax.random.randint(single_key, (N_SEQ,), 0, KVB_DEV)
        owners = jnp.arange(N_SEQ)
        first_block = jnp.where(counts == 2, low, single)
        listed = jnp.zeros((N_SEQ,), jnp.int32)
        listed = listed.at[jnp.where(counts > 0, start, N_SEQ)].set((owners * KVB_DEV + first_block).astype(jnp.int32), mode='drop')
        listed = listed.at[jnp.where(counts == 2, start + 1, N_SEQ)].set((owners * KVB_DEV + high).astype(jnp.int32), mode='drop')
        return listed
    rows = jax.vmap(one_row)(jax.random.split(key, N_GRP * N_SEQ))
    return rows.reshape(N_GRP, N_SEQ, N_SEQ)


def draw_dest(key, part):
    key = jax.random.fold_in(key, 22)

    def one_half(half_key):
        pick_key, order_key = jax.random.split(half_key)
        heavy = jax.random.randint(pick_key, (), 0, N_SEQ)
        order = jax.random.permutation(order_key, N_SEQ)
        rank = jnp.arange(N_SEQ)
        spread = (heavy + 1 + (rank - HAND) // 2 % (N_SEQ - 1)) % N_SEQ
        spread = jnp.where((rank == HAND) & (heavy != N_SEQ - 1), N_SEQ - 1, spread)
        target = jnp.where(rank < HAND, heavy, spread).astype(jnp.int32)
        return jnp.zeros((N_SEQ,), jnp.int32).at[order].set(target)
    return jax.vmap(one_half)(jax.random.split(key, N_GRP))


def draw_cache_lens(key, part):
    key = jax.random.fold_in(key, 23)
    len_key, pick_key = jax.random.split(key)
    lens = jax.random.randint(len_key, (N_GRP, N_SEQ), 1, CAP + 1)
    full = jax.random.randint(pick_key, (N_GRP, 1), 0, N_SEQ)
    return jnp.where(jnp.arange(N_SEQ)[None, :] == full, CAP, lens).astype(jnp.int32)


def set_ends(values, own_key, least, top_value):
    spot = [jax.random.randint(jax.random.fold_in(own_key, axis), (), 0, length) for axis, length in enumerate(values.shape)]
    widest = values.shape.index(max(values.shape))
    beside = spot[:widest] + [(spot[widest] + 1) % values.shape[widest]] + spot[widest + 1:]
    return values.at[tuple(spot)].set(least).at[tuple(beside)].set(top_value)


def steps_of(key, shape, shards, smallest, top_value):
    def one(dim, blocks):
        heights = jax.random.uniform(jax.random.fold_in(jax.random.fold_in(key, 6), dim), (blocks,), jnp.float32, smallest / len(shards), top_value / len(shards))
        return jnp.repeat(jnp.exp(heights), shape[dim] // blocks).reshape((-1,) + (1,) * (len(shape) - dim - 1))

    gain = one(*shards[0])
    for cut in shards[1:]:
        gain = gain * one(*cut)
    return gain


def centred(key, shape, scale, limit, cuts=(), kind=jnp.bfloat16):
    array = jax.random.normal(key, shape, jnp.float32) * scale
    if len(cuts) > 0:
        array = steps_of(key, shape, cuts, -0.22, 0.18) * array
    return jnp.clip(array, min=-limit, max=limit).astype(kind)


def setup_inputs(seed: int = 0) -> dict:
    key_of = jax.random.split(jax.random.key(seed), 14)
    return {
        "queries": draw_queries(jax.random.fold_in(key_of[13], 71), 0),
        "span_kv": draw_span_kv(jax.random.fold_in(key_of[13], 71), 0),
        "prior_kv": centred(key_of[2], (N_GRP, PRIOR, HK, 2 * DH), 1.0, 4.0, ((0, 2), (1, 32), (2, 4))),
        "list_ids": draw_list_ids(jax.random.fold_in(key_of[13], 71), 0),
        "out_weight": centred(key_of[4], (HQ * DH, DOUT), (HQ * DH // 8) ** -0.5, 0.25, ((0, 4),)),
        "pool_kv": centred(key_of[5], (N_GRP, N_SEQ, PAGES, BLK, HK, 2 * DH), 1.0, 4.0, ((0, 2), (1, 32), (4, 4))),
        "page_table": jax.vmap(lambda own: jax.random.permutation(own, PAGES))(jax.random.split(key_of[6], N_GRP * N_SEQ)).reshape((N_GRP, N_SEQ, PAGES)).astype(jnp.int32),
        "cache_lens": draw_cache_lens(jax.random.fold_in(key_of[13], 71), 0),
        "hist_kv": centred(key_of[8], (N_GRP, N_SEQ, BEAMS, HIST, HK, 2 * DH), 1.0, 4.0, ((0, 2), (1, 32), (4, 4))),
        "dec_q": draw_dec_q(jax.random.fold_in(key_of[13], 71), 0),
        "dec_kv": draw_dec_kv(jax.random.fold_in(key_of[13], 71), 0),
        "parents": set_ends(jax.random.randint(key_of[11], (N_GRP, N_SEQ, BEAMS), 0, BEAMS), jax.random.fold_in(key_of[11], 1), 0, BEAMS - 1).astype(jnp.int32),
        "dest": draw_dest(jax.random.fold_in(key_of[13], 71), 0),
    }


FLOOR = -1e30


def mix_rows(scores, allowed, values):
    scores = jnp.where(allowed, scores, FLOOR)
    top = jnp.max(scores, axis=-1, keepdims=True)
    weights = jnp.exp(scores - top)
    total = jnp.sum(weights, axis=-1, keepdims=True)
    rounded = lax.optimization_barrier(weights.astype(jnp.bfloat16)).astype(jnp.float32)
    mixed = jnp.einsum('...k,kd->...d', rounded, values.astype(jnp.float32))
    return (mixed / total).astype(jnp.bfloat16)


def prefill_one(index, queries, span_kv, prior_kv, list_ids, out_weight):
    half = index // N_SEQ
    shard = index % N_SEQ
    ask = lax.dynamic_slice_in_dim(queries[half], shard * SPAN_DEV, SPAN_DEV, 0)
    own = lax.dynamic_slice_in_dim(span_kv[half], shard * SPAN_DEV, SPAN_DEV, 0)
    blocks = prior_kv[half].reshape(PRIOR // BLK, BLK, HK, 2 * DH)
    listed = jnp.take(blocks, list_ids[half, shard], axis=0).reshape(LIST * BLK, HK, 2 * DH)
    keys_all = jnp.concatenate([listed, own], axis=0)
    token = jnp.arange(SPAN_DEV)
    allowed = jnp.concatenate([jnp.ones((SPAN_DEV, LIST * BLK), jnp.bool_), token[None, :] <= token[:, None]], axis=1)
    group = HQ // HK
    pieces = []
    for head in range(HK):
        rows = ask[:, head * group:(head + 1) * group, :].astype(jnp.float32)
        scores = jnp.einsum('tgd,kd->gtk', rows, keys_all[:, head, :DH].astype(jnp.float32)) * DH ** -0.5
        done = mix_rows(scores, allowed[None], keys_all[:, head, DH:])
        pieces.append(done.transpose(1, 0, 2))
    attended = jnp.concatenate(pieces, axis=1).reshape(SPAN_DEV, HQ * DH)
    return jnp.dot(attended, out_weight, preferred_element_type=jnp.float32).astype(jnp.bfloat16)


def beam_attend(ask, shared, shared_ok, own):
    beams = ask.shape[0]
    heads = shared.shape[1]
    ask = ask.reshape(beams, heads, HQ // heads, DH).astype(jnp.float32)
    far = jnp.einsum('bhgd,shd->bhgs', ask, shared[..., :DH].astype(jnp.float32)) * DH ** -0.5
    near = jnp.einsum('bhgd,bohd->bhgo', ask, own[..., :DH].astype(jnp.float32)) * DH ** -0.5
    far = jnp.where(shared_ok, far, FLOOR)
    top = jnp.maximum(jnp.max(far, axis=-1, keepdims=True), jnp.max(near, axis=-1, keepdims=True))
    far_w = jnp.exp(far - top)
    near_w = jnp.exp(near - top)
    total = jnp.sum(far_w, axis=-1, keepdims=True) + jnp.sum(near_w, axis=-1, keepdims=True)
    far_r = lax.optimization_barrier(far_w.astype(jnp.bfloat16)).astype(jnp.float32)
    near_r = lax.optimization_barrier(near_w.astype(jnp.bfloat16)).astype(jnp.float32)
    mixed = jnp.einsum('bhgs,shd->bhgd', far_r, shared[..., DH:].astype(jnp.float32))
    mixed = mixed + jnp.einsum('bhgo,bohd->bhgd', near_r, own[..., DH:].astype(jnp.float32))
    return (mixed / total).astype(jnp.bfloat16).reshape(beams, HQ, DH)


def decode_one(index, span_kv, pool_kv, page_table, cache_lens, hist_kv, dec_q, dec_kv, parents, dest):
    half = index // N_SEQ
    request = index % N_SEQ
    cache = jnp.take(pool_kv[half, request], page_table[half, request], axis=0).reshape(CAP, HK, 2 * DH)
    live = jnp.arange(CAP) < cache_lens[half, request]
    handed = span_kv[1 - half]
    handed_ok = jnp.repeat(dest[half] == request, SPAN_DEV)
    shared = jnp.concatenate([cache, handed], axis=0)
    shared_ok = jnp.concatenate([live, handed_ok])
    history = hist_kv[half, request]
    first = dec_kv[half, 0, request]
    second = dec_kv[half, 1, request]
    parent = parents[half, request]
    step_one = jnp.concatenate([history, first[:, None]], axis=1)
    step_two = jnp.concatenate([jnp.take(history, parent, axis=0), jnp.take(first, parent, axis=0)[:, None], second[:, None]], axis=1)
    out_one = beam_attend(dec_q[half, 0, request], shared, shared_ok, step_one)
    out_two = beam_attend(dec_q[half, 1, request], shared, shared_ok, step_two)
    return jnp.stack([out_one, out_two])


def reference(queries, span_kv, prior_kv, list_ids, out_weight, pool_kv, page_table, cache_lens, hist_kv, dec_q, dec_kv, parents, dest):
    flat = jnp.arange(N_GRP * N_SEQ, dtype=jnp.int32)
    prefill_out = lax.map(lambda index: prefill_one(index, queries, span_kv, prior_kv, list_ids, out_weight), flat)
    prefill_out = prefill_out.reshape(N_GRP, N_SEQ * SPAN_DEV, DOUT)
    decode_out = lax.map(lambda index: decode_one(index, span_kv, pool_kv, page_table, cache_lens, hist_kv, dec_q, dec_kv, parents, dest), flat)
    decode_out = decode_out.reshape(N_GRP, N_SEQ, STEPS, BEAMS, HQ, DH).transpose(0, 2, 1, 3, 4, 5)
    return prefill_out, decode_out
```

```python
import functools

import jax
import jax.numpy as jnp
from jax import lax
from jax.experimental import pallas as pl
from jax.experimental.pallas import tpu as pltpu
from jax.sharding import PartitionSpec as P

BLK = 128
SLOTS = 2
HANDED = 3
NY, NZ, NC = 4, 4, 2
PLANE = NY * NC
LOG2E = 1.4426950408889634
FLOOR = -1e30
STAT_ROWS = 16
LANES = 256


def seq_of(y, z, c):
    return (y * NZ + z) * NC + c


def planes():
    return [[seq_of(y, z, c) for y in range(NY) for c in range(NC)] for z in range(NZ)]


def z_shift(by):
    return [
        (seq_of(y, z, c), seq_of(y, (z + by) % NZ, c))
        for y in range(NY)
        for z in range(NZ)
        for c in range(NC)
    ]


def attend(tab_ref, q_ref, kv_ref, s_scr, vt_scr, m_scr, l_scr, acc_scr, span_ref=None):
    rows, dh = q_ref.shape
    scale = dh ** (-0.5) * LOG2E
    count = tab_ref[SLOTS * PLANE]
    m_scr[...] = jnp.full(m_scr.shape, FLOOR, jnp.float32)
    l_scr[...] = jnp.zeros(l_scr.shape, jnp.float32)
    acc_scr[...] = jnp.zeros(acc_scr.shape, jnp.float32)

    def score(block, k, masked):
        keys = block[:, :dh]
        vt_scr[k] = block[:, dh:].astype(jnp.float32).T.astype(jnp.bfloat16)
        for r in range(0, rows, LANES):
            part = lax.dot_general(
                keys,
                q_ref[r : r + LANES, :],
                (((1,), (1,)), ((), ())),
                preferred_element_type=jnp.float32,
            )
            if masked:
                key_pos = lax.broadcasted_iota(jnp.int32, part.shape, 0)
                tok = lax.broadcasted_iota(jnp.int32, part.shape, 1) % BLK
                part = jnp.where(key_pos <= tok, part, FLOOR)
            s_scr[k, :, r : r + LANES] = part
            top = jnp.max(part.reshape(BLK // 8, 8, LANES), axis=0)
            m_scr[:, r : r + LANES] = jnp.maximum(m_scr[:, r : r + LANES], top)

    def first(k, _):
        score(kv_ref[tab_ref[k]], k, False)
        return 0

    lax.fori_loop(0, count, first, 0)
    if span_ref is not None:
        score(span_ref[...], count, True)
        count = count + 1

    @pl.when(count % 2 == 1)
    def _():
        s_scr[count] = jnp.full(s_scr.shape[1:], FLOOR, jnp.float32)
        vt_scr[count] = jnp.zeros(vt_scr.shape[1:], vt_scr.dtype)

    top = jnp.max(m_scr[...], axis=0, keepdims=True) * scale

    def second(k, _):
        vt = jnp.concatenate([vt_scr[2 * k], vt_scr[2 * k + 1]], axis=1)
        for r in range(0, rows, LANES):
            part = s_scr[pl.ds(2 * k, 2), :, r : r + LANES].reshape(2 * BLK, LANES)
            weight = jnp.exp2(part * scale - top[:, r : r + LANES])
            l_scr[:, r : r + LANES] += jnp.sum(weight.reshape(BLK // 4, 8, LANES), axis=0)
            acc_scr[:, r : r + LANES] += jnp.dot(
                vt, weight.astype(jnp.bfloat16), preferred_element_type=jnp.float32
            )
        return 0

    lax.fori_loop(0, (count + 1) // 2, second, 0)
    total = jnp.sum(l_scr[...], axis=0, keepdims=True)
    some = total > 0.0
    safe = jnp.where(some, total, 1.0)
    lse = jnp.where(some, top + jnp.log(safe) * LOG2E, FLOOR)
    return 1.0 / safe, lse


def proxy_kernel(tab_ref, q_ref, kv_ref, out_ref, s_scr, vt_scr, m_scr, l_scr, acc_scr):
    inverse, lse = attend(tab_ref, q_ref, kv_ref, s_scr, vt_scr, m_scr, l_scr, acc_scr)
    dh = q_ref.shape[1]
    out_ref[:dh, :] = (acc_scr[...] * inverse).astype(jnp.bfloat16)
    one = lse.astype(jnp.bfloat16).astype(jnp.float32)
    two = (lse - one).astype(jnp.bfloat16).astype(jnp.float32)
    three = lse - one - two
    row = lax.broadcasted_iota(jnp.int32, (STAT_ROWS, lse.shape[1]), 0)
    stat = jnp.where(row == 0, one, jnp.where(row == 1, two, jnp.where(row == 2, three, 0.0)))
    out_ref[dh:, :] = stat.astype(jnp.bfloat16)


def scratch(rows, dh, blocks):
    return [
        pltpu.VMEM((blocks, BLK, rows), jnp.float32),
        pltpu.VMEM((blocks, dh, BLK), jnp.bfloat16),
        pltpu.VMEM((8, rows), jnp.float32),
        pltpu.VMEM((8, rows), jnp.float32),
        pltpu.VMEM((dh, rows), jnp.float32),
    ]


VMEM = functools.partial(pl.BlockSpec, memory_space=pltpu.VMEM)
SMEM = functools.partial(pl.BlockSpec, memory_space=pltpu.SMEM)


def proxy_attend(tab, q, kv):
    rows, dh = q.shape
    return pl.pallas_call(
        proxy_kernel,
        out_shape=jax.ShapeDtypeStruct((dh + STAT_ROWS, rows), jnp.bfloat16),
        in_specs=[SMEM(), VMEM(), VMEM()],
        out_specs=VMEM(),
        scratch_shapes=scratch(rows, dh, SLOTS * PLANE),
        compiler_params=pltpu.CompilerParams(vmem_limit_bytes=24 * 2**20),
        name="proxy_attend",
    )(tab, q, kv)


def final_kernel(
    tab_ref, col_ref, q_ref, kv_ref, span_ref, back1, back2, back3, w_hbm, out_ref,
    s_scr, vt_scr, m_scr, l_scr, acc_scr, w_scr, a_scr, sems,
):
    width = out_ref.shape[2]
    copies = []
    for k in range(out_ref.shape[0]):
        col = pl.multiple_of(col_ref[k] * width, width)
        copies.append(
            pltpu.make_async_copy(w_hbm.at[:, pl.ds(col, width)], w_scr.at[k], sems.at[k])
        )
        copies[-1].start()
    dh = q_ref.shape[1]
    inverse, lse = attend(tab_ref, q_ref, kv_ref, s_scr, vt_scr, m_scr, l_scr, acc_scr, span_ref)
    others = []
    for back in (back1, back2, back3):
        stat = back[dh:, :].astype(jnp.float32)
        others.append(stat[0:1] + stat[1:2] + stat[2:3])
    top = lse
    for other in others:
        top = jnp.maximum(top, other)
    own_w = jnp.exp2(lse - top)
    weights = [jnp.exp2(other - top) for other in others]
    total = own_w + weights[0] + weights[1] + weights[2]
    share = 1.0 / total
    own_w = own_w * inverse * share
    weights = [w * share for w in weights]
    for h in range(q_ref.shape[0] // BLK):
        sl = slice(h * BLK, (h + 1) * BLK)
        mixed = acc_scr[:, sl] * own_w[:, sl]
        for back, w in zip((back1, back2, back3), weights):
            mixed = mixed + back[:dh, sl].astype(jnp.float32) * w[:, sl]
        a_scr[:, h * dh : (h + 1) * dh] = mixed.T.astype(jnp.bfloat16)
    for k in range(out_ref.shape[0]):
        copies[k].wait()
        out_ref[k] = jnp.dot(
            a_scr[...], w_scr[k], preferred_element_type=jnp.float32
        ).astype(jnp.bfloat16)


def final_attend(tab, cols, q, kv, span, backs, weight):
    rows, dh = q.shape
    ntp = cols.shape[0]
    depth, wide = weight.shape
    return pl.pallas_call(
        final_kernel,
        out_shape=jax.ShapeDtypeStruct((ntp, BLK, wide // ntp), jnp.bfloat16),
        in_specs=[SMEM(), SMEM(), VMEM(), VMEM(), VMEM(), VMEM(), VMEM(), VMEM(),
                  pl.BlockSpec(memory_space=pl.ANY)],
        out_specs=VMEM(),
        scratch_shapes=scratch(rows, dh, SLOTS * PLANE + 2) + [
            pltpu.VMEM((ntp, depth, wide // ntp), jnp.bfloat16),
            pltpu.VMEM((BLK, depth), jnp.bfloat16),
            pltpu.SemaphoreType.DMA((ntp,)),
        ],
        compiler_params=pltpu.CompilerParams(vmem_limit_bytes=40 * 2**20),
        name="final_attend",
    )(tab, cols, q, kv, span, *backs, weight)


def decode_kernel(
    table_ref, meta_ref, parents_ref, q_ref, pool_ref, hand_ref, hist_ref, new_ref, out_ref, s_scr,
):
    rows, dh = q_ref.shape
    pages = pool_ref.shape[0]
    beams = hist_ref.shape[0]
    group = rows // (2 * beams)
    scale = dh ** (-0.5) * LOG2E
    length = meta_ref[0]
    n_hand = meta_ref[1]
    q = q_ref[...]
    row = lax.broadcasted_iota(jnp.int32, (rows, BLK), 0)
    lane = lax.broadcasted_iota(jnp.int32, (rows, BLK), 1)
    later = row >= rows // 2
    beam = (row // group) % beams
    parent = jnp.zeros_like(beam)
    for b in range(beams):
        parent = jnp.where(beam == b, parents_ref[b], parent)
    source = jnp.where(later, parent, beam)
    tiles = []
    for i in range(pages):
        tiles.append((functools.partial(lambda i: pool_ref[table_ref[i]], i), lane < length - i * BLK))
    piece = BLK // 32
    for i in range(HANDED):
        slot = ((lane + i * BLK) // piece) % HANDED
        tiles.append((functools.partial(lambda i: hand_ref[i * BLK : (i + 1) * BLK], i), slot < n_hand))
    for b in range(beams):
        tiles.append((functools.partial(lambda b: hist_ref[b], b), source == b))
    fresh = ((lane < beams) & (source == lane)) | (
        (lane >= beams) & (lane < 2 * beams) & later & (beam == lane - beams)
    )
    tiles.append((lambda: new_ref[...], fresh))
    top = jnp.full((rows, BLK), FLOOR, jnp.float32)
    for t, (get, allowed) in enumerate(tiles):
        part = lax.dot_general(
            q, get()[:, :dh], (((1,), (1,)), ((), ())), preferred_element_type=jnp.float32
        ) * scale
        part = jnp.where(allowed, part, FLOOR)
        s_scr[t] = part
        top = jnp.maximum(top, part)
    top = jnp.max(top, axis=1, keepdims=True)
    total = jnp.zeros((rows, BLK), jnp.float32)
    acc = jnp.zeros((rows, dh), jnp.float32)
    for t, (get, _) in enumerate(tiles):
        weight = jnp.exp2(s_scr[t] - top)
        total = total + weight
        acc = acc + jnp.dot(
            weight.astype(jnp.bfloat16), get()[:, dh:], preferred_element_type=jnp.float32
        )
    out_ref[...] = (acc / jnp.sum(total, axis=1, keepdims=True)).astype(jnp.bfloat16)


def decode_attend(table, meta, parents, q, pool, hand, hist, new):
    rows, dh = q.shape
    tiles = pool.shape[0] + HANDED + hist.shape[0] + 1
    return pl.pallas_call(
        decode_kernel,
        out_shape=jax.ShapeDtypeStruct((rows, dh), jnp.bfloat16),
        in_specs=[SMEM(), SMEM(), SMEM(), VMEM(), VMEM(), VMEM(), VMEM(), VMEM()],
        out_specs=VMEM(),
        scratch_shapes=[pltpu.VMEM((tiles, rows, BLK), jnp.float32)],
        compiler_params=pltpu.CompilerParams(vmem_limit_bytes=16 * 2**20),
        name="decode_attend",
    )(table, meta, parents, q, pool, hand, hist, new)


def local(
    queries, span_kv, prior_kv, list_ids, out_weight, pool_kv, page_table, cache_lens,
    hist_kv, dec_q, dec_kv, parents, dest,
):
    nseq = lax.axis_size("seq")
    ntp = lax.axis_size("tp")
    me = lax.axis_index("seq")
    y, z, c = me // (NZ * NC), (me // NC) % NZ, me % NC
    span_len, group, dh = queries.shape[1:]
    width = 2 * dh
    kvb = prior_kv.shape[1] // BLK
    lists = list_ids[0]
    owner = lists // kvb

    mine = owner == me
    own_id = lists % kvb
    first = jnp.min(jnp.where(mine, own_id, kvb - 1), axis=1)
    last = jnp.max(jnp.where(mine, own_id, 0), axis=1)
    pick = jnp.stack([first, last], axis=1).reshape(NY, NZ, NC, SLOTS)

    offs = [2, 1, 3, 0]
    client = jnp.stack([seq_of(y, (z + off) % NZ, c) for off in offs])
    client_owner = jnp.take(owner, client, axis=0, mode="clip")
    srcs = jnp.arange(nseq).reshape(NY, NZ, NC)
    srcs = lax.dynamic_index_in_dim(srcs, z, 1, keepdims=False).reshape(PLANE)
    count = jnp.sum(client_owner[:, None, :] == srcs[None, :, None], axis=2)
    valid = (jnp.arange(SLOTS)[None, None, :] < count[:, :, None]).reshape(len(offs), -1)
    place = jnp.sum(
        valid[:, None, :] & (jnp.arange(SLOTS * PLANE)[None, :] < jnp.arange(SLOTS * PLANE)[:, None])[None],
        axis=2,
    )
    at = valid[:, None, :] & (place[:, None, :] == jnp.arange(SLOTS * PLANE)[None, :, None])
    order = jnp.sum(jnp.where(at, jnp.arange(SLOTS * PLANE)[None, None, :], 0), axis=2)
    tabs = jnp.concatenate([order, jnp.sum(count, axis=1)[:, None]], axis=1).astype(jnp.int32)

    blocks = prior_kv.reshape(kvb, BLK, width)
    arrived = {}
    for i, off in enumerate(offs):
        picked = lax.dynamic_index_in_dim(pick, (z + off) % NZ, 1, keepdims=False).reshape(-1)
        outgoing = blocks.at[picked].get(mode="promise_in_bounds")
        arrived[off] = lax.all_to_all(
            outgoing.reshape(PLANE, SLOTS, BLK, width), "seq", 0, 0, tiled=True,
            axis_index_groups=planes(),
        ).reshape(PLANE * SLOTS, BLK, width)

    ask = queries[0].transpose(1, 0, 2).reshape(group * span_len, dh)
    backs = []
    for i, off in enumerate(offs[:-1]):
        there = lax.ppermute(ask, "seq", z_shift(-off))
        part = proxy_attend(tabs[i], there, arrived[off])
        backs.append(lax.ppermute(part, "seq", z_shift(off)))

    here = lax.ppermute(span_kv.reshape(span_len, width), "grp", [(0, 1), (1, 0)])
    piece = lax.all_to_all(here.reshape(nseq, span_len // nseq, width), "seq", 0, 0, tiled=True)
    goal = dest[0]
    rank = jnp.sum(
        (goal[None, :] == goal[:, None]) & (jnp.arange(nseq)[None, :] < jnp.arange(nseq)[:, None]), axis=1
    )
    sent = (goal[None, None, :] == jnp.arange(nseq)[:, None, None]) & (
        rank[None, None, :] == jnp.arange(HANDED)[None, :, None]
    )
    which = jnp.sum(jnp.where(sent, jnp.arange(nseq)[None, None, :], 0), axis=2).reshape(-1)
    pieces = piece.at[which].get(mode="promise_in_bounds")
    handed = lax.all_to_all(
        pieces.reshape(nseq, HANDED, span_len // nseq, width), "seq", 0, 0, tiled=True
    ).reshape(HANDED * span_len, width)
    n_hand = jnp.sum(goal == me)

    beams = hist_kv.shape[2]
    steps = dec_q.shape[1]
    new = dec_kv.reshape(steps * beams, width)
    new = jnp.concatenate([new, jnp.zeros((BLK - steps * beams, width), new.dtype)], axis=0)
    meta = jnp.stack([cache_lens[0, 0], n_hand]).astype(jnp.int32)
    decoded = decode_attend(
        page_table[0, 0], meta, parents[0, 0], dec_q.reshape(steps * beams * group, dh),
        pool_kv.reshape(-1, BLK, width), handed, hist_kv.reshape(beams, -1, width), new,
    )

    tp = lax.axis_index("tp")
    cols = jnp.stack([(tp + off) % ntp for off in range(ntp)]).astype(jnp.int32)
    parts = final_attend(
        tabs[-1], cols, ask, arrived[0], span_kv.reshape(span_len, width), backs, out_weight
    )
    summed = parts[0].astype(jnp.float32)
    for off in (2, 1, 3):
        got = lax.ppermute(parts[off], "tp", [(i, (i + off) % ntp) for i in range(ntp)])
        summed = summed + got.astype(jnp.float32)
    return summed.astype(jnp.bfloat16)[None], decoded.reshape(dec_q.shape)


def solution(mesh):
    return jax.shard_map(
        local,
        mesh=mesh,
        in_specs=(
            P("grp", "seq", "tp", None),
            P("grp", "seq", "tp", None),
            P("grp", "seq", "tp", None),
            P("grp", None, None),
            P("tp", None),
            P("grp", "seq", None, None, "tp", None),
            P("grp", "seq", None),
            P("grp", "seq"),
            P("grp", "seq", None, None, "tp", None),
            P("grp", None, "seq", None, "tp", None),
            P("grp", None, "seq", None, "tp", None),
            P("grp", "seq", None),
            P("grp", None),
        ),
        out_specs=(P("grp", "seq", "tp"), P("grp", None, "seq", None, "tp", None)),
        check_vma=False,
    )
```

```python
import functools

import jax
import jax.numpy as jnp
from jax import lax
from jax.experimental import pallas as pl
from jax.experimental.pallas import tpu as pltpu
from jax.sharding import PartitionSpec as P

BLK = 128
SLOTS = 2
HANDED = 3
NY, NZ, NC = 4, 4, 2
PLANE = NY * NC
PIECE = BLK // PLANE
LOG2E = 1.4426950408889634
FLOOR = -1e30
STAT_ROWS = 16
LANES = 256


def seq_of(y, z, c):
    return (y * NZ + z) * NC + c


def planes():
    return [[seq_of(y, z, c) for y in range(NY) for c in range(NC)] for z in range(NZ)]


def z_shift(by):
    return [
        (seq_of(y, z, c), seq_of(y, (z + by) % NZ, c))
        for y in range(NY)
        for z in range(NZ)
        for c in range(NC)
    ]


def attend(
    base, tab_ref, q_ref, kv_hbm, s_scr, vt_scr, m_scr, l_scr, acc_scr, kv_scr, kv_sem, span_ref=None
):
    rows, dh = q_ref.shape
    scale = dh ** (-0.5) * LOG2E
    count = tab_ref[SLOTS * PLANE]

    def fetch(k):
        at = tab_ref[k]
        start = pl.multiple_of(base + (at % SLOTS) * BLK, BLK)
        return pltpu.make_async_copy(
            kv_hbm.at[at // SLOTS, pl.ds(start, BLK), :], kv_scr.at[k], kv_sem.at[k]
        )

    def begin(k, _):
        fetch(k).start()
        return 0

    lax.fori_loop(0, count, begin, 0)
    m_scr[...] = jnp.full(m_scr.shape, FLOOR, jnp.float32)
    l_scr[...] = jnp.zeros(l_scr.shape, jnp.float32)
    acc_scr[...] = jnp.zeros(acc_scr.shape, jnp.float32)

    def score(block, k, masked):
        keys = block[:, :dh]
        vt_scr[k] = block[:, dh:].astype(jnp.float32).T.astype(jnp.bfloat16)
        for r in range(0, rows, LANES):
            part = lax.dot_general(
                keys,
                q_ref[r : r + LANES, :],
                (((1,), (1,)), ((), ())),
                preferred_element_type=jnp.float32,
            )
            if masked:
                key_pos = lax.broadcasted_iota(jnp.int32, part.shape, 0)
                tok = lax.broadcasted_iota(jnp.int32, part.shape, 1) % BLK
                part = jnp.where(key_pos <= tok, part, FLOOR)
            s_scr[k, :, r : r + LANES] = part
            top = jnp.max(part.reshape(BLK // 8, 8, LANES), axis=0)
            m_scr[:, r : r + LANES] = jnp.maximum(m_scr[:, r : r + LANES], top)

    def first(k, _):
        fetch(k).wait()
        score(kv_scr[k], k, False)
        return 0

    lax.fori_loop(0, count, first, 0)
    if span_ref is not None:
        score(span_ref[...], count, True)
        count = count + 1

    @pl.when(count % 2 == 1)
    def _():
        s_scr[count] = jnp.full(s_scr.shape[1:], FLOOR, jnp.float32)
        vt_scr[count] = jnp.zeros(vt_scr.shape[1:], vt_scr.dtype)

    top = jnp.max(m_scr[...], axis=0, keepdims=True) * scale

    def second(k, _):
        vt = jnp.concatenate([vt_scr[2 * k], vt_scr[2 * k + 1]], axis=1)
        for r in range(0, rows, LANES):
            part = s_scr[pl.ds(2 * k, 2), :, r : r + LANES].reshape(2 * BLK, LANES)
            weight = jnp.exp2(part * scale - top[:, r : r + LANES])
            l_scr[:, r : r + LANES] += jnp.sum(weight.reshape(BLK // 4, 8, LANES), axis=0)
            acc_scr[:, r : r + LANES] += jnp.dot(
                vt, weight.astype(jnp.bfloat16), preferred_element_type=jnp.float32
            )
        return 0

    lax.fori_loop(0, (count + 1) // 2, second, 0)
    total = jnp.sum(l_scr[...], axis=0, keepdims=True)
    some = total > 0.0
    safe = jnp.where(some, total, 1.0)
    lse = jnp.where(some, top + jnp.log(safe) * LOG2E, FLOOR)
    return 1.0 / safe, lse


def proxy_kernel(base, own, tab_ref, q_ref, kv_hbm, *rest):
    span_ref, rest = (rest[0], rest[1:]) if own else (None, rest)
    out_ref, scr = rest[0], rest[1:]
    inverse, lse = attend(base, tab_ref, q_ref, kv_hbm, *scr, span_ref)
    acc_scr = scr[4]
    dh = q_ref.shape[1]
    out_ref[:dh, :] = (acc_scr[...] * inverse).astype(jnp.bfloat16)
    one = lse.astype(jnp.bfloat16).astype(jnp.float32)
    two = (lse - one).astype(jnp.bfloat16).astype(jnp.float32)
    three = lse - one - two
    row = lax.broadcasted_iota(jnp.int32, (STAT_ROWS, lse.shape[1]), 0)
    stat = jnp.where(row == 0, one, jnp.where(row == 1, two, jnp.where(row == 2, three, 0.0)))
    out_ref[dh:, :] = stat.astype(jnp.bfloat16)


def scratch(rows, dh, blocks):
    return [
        pltpu.VMEM((blocks, BLK, rows), jnp.float32),
        pltpu.VMEM((blocks, dh, BLK), jnp.bfloat16),
        pltpu.VMEM((8, rows), jnp.float32),
        pltpu.VMEM((8, rows), jnp.float32),
        pltpu.VMEM((dh, rows), jnp.float32),
        pltpu.VMEM((SLOTS * PLANE, BLK, 2 * dh), jnp.bfloat16),
        pltpu.SemaphoreType.DMA((SLOTS * PLANE,)),
    ]


VMEM = functools.partial(pl.BlockSpec, memory_space=pltpu.VMEM)
SMEM = functools.partial(pl.BlockSpec, memory_space=pltpu.SMEM)
ANY = functools.partial(pl.BlockSpec, memory_space=pl.ANY)
HBM = functools.partial(pl.BlockSpec, memory_space=pltpu.HBM)


def pack_kernel(groups, extra, pick_ref, blocks, more, *rest):
    if extra == "table":
        which_ref, out, stage, sems_in, sems_out = rest
    else:
        out, stage, sems_in, sems_out = rest
    pairs = []

    def send(src, place):
        k = len(pairs)
        arrive = pltpu.make_async_copy(src, place(stage), sems_in.at[k])
        arrive.start()
        pairs.append((arrive, pltpu.make_async_copy(place(stage), place(out), sems_out.at[k])))

    each = groups * SLOTS
    rows = each * BLK
    for p in range(PLANE):
        for s in range(each):
            send(blocks.at[pick_ref[p * each + s]], lambda ref, p=p, s=s: ref.at[p, pl.ds(s * BLK, BLK), :])
    if extra == "pieces":
        for p in range(PLANE):
            send(more.at[p], lambda ref, p=p: ref.at[p, pl.ds(rows, PIECE), :])
    if extra == "table":
        for p in range(PLANE):
            for s in range(HANDED):
                send(
                    more.at[which_ref[p * HANDED + s]],
                    lambda ref, p=p, s=s: ref.at[p, pl.ds(rows + s * PIECE, PIECE), :],
                )
    for arrive, leave in pairs:
        arrive.wait()
        leave.start()
    for _, leave in pairs:
        leave.wait()


def pack(blocks, pick, groups, extra=None, more=None, which=None):
    width = blocks.shape[2]
    rows = groups * SLOTS * BLK + {None: 0, "pieces": PIECE, "table": HANDED * PIECE}[extra]
    count = groups * SLOTS * PLANE + {None: 0, "pieces": PLANE, "table": HANDED * PLANE}[extra]
    if more is None:
        more = jnp.zeros((8, 128), jnp.bfloat16)
    blocks = pltpu.with_memory_space_constraint(blocks, pltpu.HBM)
    args = [pick, blocks, more] + ([which] if extra == "table" else [])
    specs = [SMEM(), HBM(), ANY()] + ([SMEM()] if extra == "table" else [])
    return pl.pallas_call(
        functools.partial(pack_kernel, groups, extra),
        out_shape=pltpu.HBM((PLANE, rows, width), jnp.bfloat16),
        in_specs=specs,
        out_specs=HBM(),
        scratch_shapes=[
            pltpu.VMEM((PLANE, rows, width), jnp.bfloat16),
            pltpu.SemaphoreType.DMA((count,)),
            pltpu.SemaphoreType.DMA((count,)),
        ],
        compiler_params=pltpu.CompilerParams(vmem_limit_bytes=16 * 2**20),
        name="pack",
    )(*args)


def proxy_attend(tab, q, kv, base, span=None):
    rows, dh = q.shape
    own = span is not None
    return pl.pallas_call(
        functools.partial(proxy_kernel, base, own),
        out_shape=jax.ShapeDtypeStruct((dh + STAT_ROWS, rows), jnp.bfloat16),
        in_specs=[SMEM(), VMEM(), ANY()] + [VMEM()] * own,
        out_specs=VMEM(),
        scratch_shapes=scratch(rows, dh, SLOTS * PLANE + 2 * own),
        compiler_params=pltpu.CompilerParams(vmem_limit_bytes=24 * 2**20),
        name="proxy_attend",
    )(tab, q, kv, *([span] if own else []))


def final_kernel(col_ref, part1, part2, part3, part4, w_hbm, out1, out2, out3, out4, w_scr, a_scr, sems):
    outs = (out1, out2, out3, out4)
    parts = (part1, part2, part3, part4)
    width = out1.shape[1]
    copies = []
    for k in range(len(outs)):
        col = pl.multiple_of(col_ref[k] * width, width)
        copies.append(
            pltpu.make_async_copy(w_hbm.at[:, pl.ds(col, width)], w_scr.at[k], sems.at[k])
        )
        copies[-1].start()
    rows = part1.shape[1]
    dh = part1.shape[0] - STAT_ROWS
    lses = []
    for part in parts:
        stat = part[dh:, :].astype(jnp.float32)
        lses.append(stat[0:1] + stat[1:2] + stat[2:3])
    top = functools.reduce(jnp.maximum, lses)
    weights = [jnp.exp2(lse - top) for lse in lses]
    share = 1.0 / functools.reduce(jnp.add, weights)
    weights = [w * share for w in weights]
    for h in range(rows // BLK):
        sl = slice(h * BLK, (h + 1) * BLK)
        mixed = functools.reduce(
            jnp.add, [part[:dh, sl].astype(jnp.float32) * w[:, sl] for part, w in zip(parts, weights)]
        )
        a_scr[:, h * dh : (h + 1) * dh] = mixed.T.astype(jnp.bfloat16)
    for k, out in enumerate(outs):
        copies[k].wait()
        out[...] = jnp.dot(
            a_scr[...], w_scr[k], preferred_element_type=jnp.float32
        ).astype(jnp.bfloat16)


def final_project(cols, parts, weight):
    ntp = cols.shape[0]
    depth, wide = weight.shape
    return pl.pallas_call(
        final_kernel,
        out_shape=[jax.ShapeDtypeStruct((BLK, wide // ntp), jnp.bfloat16)] * ntp,
        in_specs=[SMEM()] + [VMEM()] * len(parts) + [HBM()],
        out_specs=[VMEM()] * ntp,
        scratch_shapes=[
            pltpu.VMEM((ntp, depth, wide // ntp), jnp.bfloat16),
            pltpu.VMEM((BLK, depth), jnp.bfloat16),
            pltpu.SemaphoreType.DMA((ntp,)),
        ],
        compiler_params=pltpu.CompilerParams(vmem_limit_bytes=24 * 2**20),
        name="final_project",
    )(cols, *parts, pltpu.with_memory_space_constraint(weight, pltpu.HBM))


def decode_kernel(
    table_ref, meta_ref, parents_ref, q_ref, pool_ref, hand_ref, hist_ref, new_ref, out_ref, s_scr,
):
    rows, dh = q_ref.shape
    pages = pool_ref.shape[0]
    beams = hist_ref.shape[0]
    group = rows // (2 * beams)
    scale = dh ** (-0.5) * LOG2E
    length = meta_ref[0]
    n_hand = meta_ref[1]
    q = q_ref[...]
    row = lax.broadcasted_iota(jnp.int32, (rows, BLK), 0)
    lane = lax.broadcasted_iota(jnp.int32, (rows, BLK), 1)
    later = row >= rows // 2
    beam = (row // group) % beams
    parent = jnp.zeros_like(beam)
    for b in range(beams):
        parent = jnp.where(beam == b, parents_ref[b], parent)
    source = jnp.where(later, parent, beam)
    tiles = []
    for i in range(pages):
        tiles.append((functools.partial(lambda i: pool_ref[table_ref[i]], i), lane < length - i * BLK))
    for i in range(HANDED):
        slot = ((lane + i * BLK) // PIECE) % HANDED
        tiles.append((functools.partial(lambda i: hand_ref[i * BLK : (i + 1) * BLK], i), slot < n_hand))
    for b in range(beams):
        tiles.append((functools.partial(lambda b: hist_ref[b], b), source == b))
    fresh = ((lane < beams) & (source == lane)) | (
        (lane >= beams) & (lane < 2 * beams) & later & (beam == lane - beams)
    )
    tiles.append((lambda: new_ref[...], fresh))
    top = jnp.full((rows, BLK), FLOOR, jnp.float32)
    for t, (get, allowed) in enumerate(tiles):
        part = lax.dot_general(
            q, get()[:, :dh], (((1,), (1,)), ((), ())), preferred_element_type=jnp.float32
        ) * scale
        part = jnp.where(allowed, part, FLOOR)
        s_scr[t] = part
        top = jnp.maximum(top, part)
    top = jnp.max(top, axis=1, keepdims=True)
    total = jnp.zeros((rows, BLK), jnp.float32)
    acc = jnp.zeros((rows, dh), jnp.float32)
    for t, (get, _) in enumerate(tiles):
        weight = jnp.exp2(s_scr[t] - top)
        total = total + weight
        acc = acc + jnp.dot(
            weight.astype(jnp.bfloat16), get()[:, dh:], preferred_element_type=jnp.float32
        )
    out_ref[...] = (acc / jnp.sum(total, axis=1, keepdims=True)).astype(jnp.bfloat16)


def decode_attend(table, meta, parents, q, pool, hand, hist, new):
    rows, dh = q.shape
    tiles = pool.shape[0] + HANDED + hist.shape[0] + 1
    return pl.pallas_call(
        decode_kernel,
        out_shape=jax.ShapeDtypeStruct((rows, dh), jnp.bfloat16),
        in_specs=[SMEM(), SMEM(), SMEM(), VMEM(), VMEM(), VMEM(), VMEM(), VMEM()],
        out_specs=VMEM(),
        scratch_shapes=[pltpu.VMEM((tiles, rows, BLK), jnp.float32)],
        compiler_params=pltpu.CompilerParams(vmem_limit_bytes=16 * 2**20),
        name="decode_attend",
    )(table, meta, parents, q, pool, hand, hist, new)


def local(
    queries, span_kv, prior_kv, list_ids, out_weight, pool_kv, page_table, cache_lens,
    hist_kv, dec_q, dec_kv, parents, dest,
):
    nseq = lax.axis_size("seq")
    ntp = lax.axis_size("tp")
    me = lax.axis_index("seq")
    y, z, c = me // (NZ * NC), (me // NC) % NZ, me % NC
    span_len, group, dh = queries.shape[1:]
    width = 2 * dh
    kvb = prior_kv.shape[1] // BLK
    lists = list_ids[0]
    owner = lists // kvb

    mine = owner == me
    own_id = lists % kvb
    first = jnp.min(jnp.where(mine, own_id, kvb - 1), axis=1)
    last = jnp.max(jnp.where(mine, own_id, 0), axis=1)
    pick = jnp.stack([first, last], axis=1).reshape(NY, NZ, NC, SLOTS)

    offs = [2, 1, 3, 0]
    client = jnp.stack([seq_of(y, (z + off) % NZ, c) for off in offs])
    client_owner = jnp.take(owner, client, axis=0, mode="clip")
    srcs = jnp.arange(nseq).reshape(NY, NZ, NC)
    srcs = lax.dynamic_index_in_dim(srcs, z, 1, keepdims=False).reshape(PLANE)
    count = jnp.sum(client_owner[:, None, :] == srcs[None, :, None], axis=2)
    valid = (jnp.arange(SLOTS)[None, None, :] < count[:, :, None]).reshape(len(offs), -1)
    place = jnp.sum(
        valid[:, None, :] & (jnp.arange(SLOTS * PLANE)[None, :] < jnp.arange(SLOTS * PLANE)[:, None])[None],
        axis=2,
    )
    at = valid[:, None, :] & (place[:, None, :] == jnp.arange(SLOTS * PLANE)[None, :, None])
    order = jnp.sum(jnp.where(at, jnp.arange(SLOTS * PLANE)[None, None, :], 0), axis=2)
    tabs = jnp.concatenate([order, jnp.sum(count, axis=1)[:, None]], axis=1).astype(jnp.int32)

    blocks = prior_kv.reshape(kvb, BLK, width)
    span = span_kv.reshape(span_len, width)

    def picked(*offs):
        group = [lax.dynamic_index_in_dim(pick, (z + off) % NZ, 1, keepdims=False) for off in offs]
        return jnp.concatenate(group, axis=2).reshape(-1).astype(jnp.int32)

    def exchange(message):
        return lax.all_to_all(message, "seq", 0, 0, tiled=True, axis_index_groups=planes())

    def after(value, *others):
        return lax.optimization_barrier((value,) + others)[0]

    goal = dest[0]
    rank = jnp.sum(
        (goal[None, :] == goal[:, None]) & (jnp.arange(nseq)[None, :] < jnp.arange(nseq)[:, None]), axis=1
    )
    spots = jnp.arange(nseq)
    held = ((spots // NC) % NZ - z) % NZ * PLANE + spots // (NZ * NC) * NC + spots % NC
    sent = (goal[None, None, :] == srcs[:, None, None]) & (
        rank[None, None, :] == jnp.arange(HANDED)[None, :, None]
    )
    which = jnp.sum(jnp.where(sent, held[None, None, :], 0), axis=2).reshape(-1).astype(jnp.int32)
    n_hand = jnp.sum(goal == me)

    ask = queries[0].transpose(1, 0, 2).reshape(group * span_len, dh)
    here = lax.ppermute(span, "grp", [(0, 1), (1, 0)])
    there = {off: lax.ppermute(ask, "seq", z_shift(-off)) for off in (2, 1, 3)}
    message = pack(blocks, picked(2), 1, "pieces", here.reshape(PLANE, PIECE, width))
    far = exchange(message)
    pieces = far[:, SLOTS * BLK :, :]
    pieces = [pieces] + [lax.ppermute(pieces, "seq", z_shift(-off)) for off in (1, 2, 3)]
    message = pack(blocks, picked(1, 3), 2)
    near = exchange(after(message, far, there[2]))
    part = proxy_attend(tabs[0], there[2], far, 0)
    backs = [lax.ppermute(after(part, *pieces), "seq", z_shift(2))]
    message = pack(blocks, picked(0), 1, "table", jnp.concatenate(pieces, axis=0), which)
    own = exchange(after(message, near, backs[0], there[1], there[3]))
    for i, off in enumerate((1, 3)):
        part = proxy_attend(tabs[1 + i], there[off], near, i * SLOTS * BLK)
        backs.append(lax.ppermute(part, "seq", z_shift(off)))
    handed = own[:, SLOTS * BLK :, :].reshape(HANDED * span_len, width)

    beams = hist_kv.shape[2]
    steps = dec_q.shape[1]
    new = dec_kv.reshape(steps * beams, width)
    new = jnp.concatenate([new, jnp.zeros((BLK - steps * beams, width), new.dtype)], axis=0)
    meta = jnp.stack([cache_lens[0, 0], n_hand]).astype(jnp.int32)
    decoded = decode_attend(
        page_table[0, 0], meta, parents[0, 0], dec_q.reshape(steps * beams * group, dh),
        pool_kv.reshape(-1, BLK, width), handed, hist_kv.reshape(beams, -1, width), new,
    )

    tp = lax.axis_index("tp")
    backs.append(proxy_attend(tabs[3], ask, own, 0, span))
    offsets = (2, 1, 3, 0)
    cols = jnp.stack([(tp + off) % ntp for off in offsets]).astype(jnp.int32)
    outs = final_project(cols, backs, out_weight)
    summed = outs[-1].astype(jnp.float32)
    for off, out in zip(offsets[:-1], outs):
        got = lax.ppermute(out, "tp", [(i, (i + off) % ntp) for i in range(ntp)])
        summed = summed + got.astype(jnp.float32)
    return summed.astype(jnp.bfloat16)[None], decoded.reshape(dec_q.shape)


def solution(mesh):
    return jax.shard_map(
        local,
        mesh=mesh,
        in_specs=(
            P("grp", "seq", "tp", None),
            P("grp", "seq", "tp", None),
            P("grp", "seq", "tp", None),
            P("grp", None, None),
            P("tp", None),
            P("grp", "seq", None, None, "tp", None),
            P("grp", "seq", None),
            P("grp", "seq"),
            P("grp", "seq", None, None, "tp", None),
            P("grp", None, "seq", None, "tp", None),
            P("grp", None, "seq", None, "tp", None),
            P("grp", "seq", None),
            P("grp", None),
        ),
        out_specs=(P("grp", "seq", "tp"), P("grp", None, "seq", None, "tp", None)),
        check_vma=False,
    )
```

```python
import functools

import jax
import jax.numpy as jnp
from jax import lax
from jax.experimental import pallas as pl
from jax.experimental.pallas import tpu as pltpu
from jax.sharding import PartitionSpec as P

BLK = 128
SLOTS = 2
HANDED = 3
NY, NZ, NC = 4, 4, 2
PLANE = NY * NC
PIECE = BLK // PLANE
LOG2E = 1.4426950408889634
FLOOR = -1e30
STAT_ROWS = 32
ROWS = 512


def seq_of(y, z, c):
    return (y * NZ + z) * NC + c


def planes():
    return [[seq_of(y, z, c) for y in range(NY) for c in range(NC)] for z in range(NZ)]


def z_shift(by):
    return [
        (seq_of(y, z, c), seq_of(y, (z + by) % NZ, c))
        for y in range(NY)
        for z in range(NZ)
        for c in range(NC)
    ]


VMEM = functools.partial(pl.BlockSpec, memory_space=pltpu.VMEM)
SMEM = functools.partial(pl.BlockSpec, memory_space=pltpu.SMEM)
ANY = functools.partial(pl.BlockSpec, memory_space=pl.ANY)
HBM = functools.partial(pl.BlockSpec, memory_space=pltpu.HBM)


def pack_kernel(groups, extra, pick_ref, blocks, more, *rest):
    if extra == "table":
        which_ref, out, stage, sems_in, sems_out = rest
    else:
        out, stage, sems_in, sems_out = rest
    pairs = []

    def send(src, place):
        k = len(pairs)
        arrive = pltpu.make_async_copy(src, place(stage), sems_in.at[k])
        arrive.start()
        pairs.append((arrive, pltpu.make_async_copy(place(stage), place(out), sems_out.at[k])))

    each = groups * SLOTS
    rows = each * BLK
    for p in range(PLANE):
        for s in range(each):
            send(blocks.at[pick_ref[p * each + s]], lambda ref, p=p, s=s: ref.at[p, pl.ds(s * BLK, BLK), :])
    if extra == "pieces":
        for p in range(PLANE):
            send(more.at[p], lambda ref, p=p: ref.at[p, pl.ds(rows, PIECE), :])
    if extra == "table":
        for p in range(PLANE):
            for s in range(HANDED):
                send(
                    more.at[which_ref[p * HANDED + s]],
                    lambda ref, p=p, s=s: ref.at[p, pl.ds(rows + s * PIECE, PIECE), :],
                )
    for arrive, leave in pairs:
        arrive.wait()
        leave.start()
    for _, leave in pairs:
        leave.wait()


def pack(blocks, pick, groups, extra=None, more=None, which=None):
    width = blocks.shape[2]
    rows = groups * SLOTS * BLK + {None: 0, "pieces": PIECE, "table": HANDED * PIECE}[extra]
    count = groups * SLOTS * PLANE + {None: 0, "pieces": PLANE, "table": HANDED * PLANE}[extra]
    if more is None:
        more = jnp.zeros((8, 128), jnp.bfloat16)
    blocks = pltpu.with_memory_space_constraint(blocks, pltpu.HBM)
    args = [pick, blocks, more] + ([which] if extra == "table" else [])
    specs = [SMEM(), HBM(), ANY()] + ([SMEM()] if extra == "table" else [])
    return pl.pallas_call(
        functools.partial(pack_kernel, groups, extra),
        out_shape=pltpu.HBM((PLANE, rows, width), jnp.bfloat16),
        in_specs=specs,
        out_specs=HBM(),
        scratch_shapes=[
            pltpu.VMEM((PLANE, rows, width), jnp.bfloat16),
            pltpu.SemaphoreType.DMA((count,)),
            pltpu.SemaphoreType.DMA((count,)),
        ],
        compiler_params=pltpu.CompilerParams(vmem_limit_bytes=16 * 2**20),
        name="pack",
    )(*args)


def chunks(count, body):
    def four(k, _):
        body(4 * k, 4)
        return 0

    lax.fori_loop(0, count // 4, four, 0)

    @pl.when(count % 4 >= 2)
    def _():
        body(count // 4 * 4, 2)

    @pl.when(count % 2 == 1)
    def _():
        body(count - 1, 1)


def proxy_kernel(base, own, tab_ref, q_ref, kv_ref, *rest):
    if own:
        span_ref, col_ref, w_hbm, out_ref, w_ref, s_scr, m_scr, l_scr, acc_scr, k_scr, v_scr, sems = rest
        copies = []
        width = w_ref.shape[2]
        for i in range(w_ref.shape[0]):
            col = pl.multiple_of(col_ref[i] * width, width)
            copies.append(pltpu.make_async_copy(w_hbm.at[:, pl.ds(col, width)], w_ref.at[i], sems.at[i]))
            copies[-1].start()
    else:
        out_ref, s_scr, m_scr, l_scr, acc_scr, k_scr, v_scr = rest
    rows, dh = q_ref.shape
    scale = dh ** (-0.5) * LOG2E
    count = tab_ref[SLOTS * PLANE]
    m_scr[...] = jnp.full(m_scr.shape, FLOOR, jnp.float32)
    l_scr[...] = jnp.zeros(l_scr.shape, jnp.float32)
    acc_scr[...] = jnp.zeros(acc_scr.shape, jnp.float32)

    def score(k, many, mask=None):
        keys = k_scr[pl.ds(k, many)].reshape(many * BLK, dh)
        for r in range(0, rows, ROWS):
            part = lax.dot_general(
                q_ref[r : r + ROWS, :], keys, (((1,), (1,)), ((), ())), preferred_element_type=jnp.float32
            )
            if mask is not None:
                part = jnp.where(mask, part, FLOOR)
            top = m_scr[r : r + ROWS, :]
            for i in range(many):
                piece = part[:, i * BLK : (i + 1) * BLK]
                s_scr[k + i, r : r + ROWS, :] = piece
                top = jnp.maximum(top, piece)
            m_scr[r : r + ROWS, :] = top

    def first(k, many):
        for i in range(many):
            at = tab_ref[k + i]
            start = pl.multiple_of(base + (at % SLOTS) * BLK, BLK)
            block = kv_ref[at // SLOTS, pl.ds(start, BLK), :]
            k_scr[k + i] = block[:, :dh]
            v_scr[k + i] = block[:, dh:]
        score(k, many)

    chunks(count, first)
    if own:
        k_scr[count] = span_ref[:, :dh]
        v_scr[count] = span_ref[:, dh:]
        tok = lax.broadcasted_iota(jnp.int32, (ROWS, BLK), 0) % BLK
        key = lax.broadcasted_iota(jnp.int32, (ROWS, BLK), 1)
        score(count, 1, key <= tok)
        count = count + 1
    for r in range(0, rows, ROWS):
        top = jnp.max(m_scr[r : r + ROWS, :], axis=1, keepdims=True) * scale
        m_scr[r : r + ROWS, :] = jnp.broadcast_to(top, (ROWS, BLK))

    def mix(k, many):
        values = v_scr[pl.ds(k, many)].reshape(many * BLK, dh)
        for r in range(0, rows, ROWS):
            top = m_scr[r : r + ROWS, :]
            weights = [jnp.exp2(s_scr[k + i, r : r + ROWS, :] * scale - top) for i in range(many)]
            l_scr[r : r + ROWS, :] += functools.reduce(jnp.add, weights)
            weight = jnp.concatenate([w.astype(jnp.bfloat16) for w in weights], axis=1)
            acc_scr[r : r + ROWS, :] += jnp.dot(weight, values, preferred_element_type=jnp.float32)

    chunks(count, mix)
    heads = rows // BLK
    row = lax.broadcasted_iota(jnp.int32, (heads, BLK), 0)
    lse = jnp.zeros((heads, BLK), jnp.float32)
    for h in range(heads):
        sl = slice(h * BLK, (h + 1) * BLK)
        total = jnp.broadcast_to(jnp.sum(l_scr[sl, :], axis=1, keepdims=True), (BLK, BLK))
        some = total > 0.0
        safe = jnp.where(some, total, 1.0)
        out_ref[sl, :] = (acc_scr[sl, :] * (1.0 / safe)).astype(jnp.bfloat16)
        col = jnp.where(some, m_scr[sl, :] + jnp.log(safe) * LOG2E, FLOOR)
        lse = jnp.where(row == h, col.T[:heads, :], lse)
    one = lse.astype(jnp.bfloat16).astype(jnp.float32)
    two = (lse - one).astype(jnp.bfloat16).astype(jnp.float32)
    stat = jnp.concatenate([one, two, lse - one - two, jnp.zeros_like(lse)], axis=0)
    out_ref[rows:, :] = stat.astype(jnp.bfloat16)
    if own:
        for copy in copies:
            copy.wait()


def proxy_attend(tab, q, kv, base, span=None, cols=None, weight=None):
    rows, dh = q.shape
    own = span is not None
    blocks = SLOTS * PLANE + own
    kv = pltpu.with_memory_space_constraint(kv, pltpu.VMEM)
    out_shape = [jax.ShapeDtypeStruct((rows + STAT_ROWS, dh), jnp.bfloat16)]
    args, specs, sems = [tab, q, kv], [SMEM(), VMEM(), VMEM()], []
    if own:
        ntp = cols.shape[0]
        out_shape.append(pltpu.VMEM((ntp, weight.shape[0], weight.shape[1] // ntp), jnp.bfloat16))
        args += [span, cols, pltpu.with_memory_space_constraint(weight, pltpu.HBM)]
        specs += [VMEM(), SMEM(), HBM()]
        sems = [pltpu.SemaphoreType.DMA((ntp,))]
    return pl.pallas_call(
        functools.partial(proxy_kernel, base, own),
        out_shape=out_shape,
        in_specs=specs,
        out_specs=[VMEM()] * len(out_shape),
        scratch_shapes=[
            pltpu.VMEM((blocks, rows, BLK), jnp.float32),
            pltpu.VMEM((rows, BLK), jnp.float32),
            pltpu.VMEM((rows, BLK), jnp.float32),
            pltpu.VMEM((rows, dh), jnp.float32),
            pltpu.VMEM((blocks, BLK, dh), jnp.bfloat16),
            pltpu.VMEM((blocks, BLK, dh), jnp.bfloat16),
        ] + sems,
        compiler_params=pltpu.CompilerParams(vmem_limit_bytes=28 * 2**20),
        name="proxy_attend",
    )(*args)


def merge_kernel(part1, part2, part3, part4, w_ref, a_ref, out_ref):
    parts = (part1, part2, part3, part4)
    dh = part1.shape[1]
    rows = part1.shape[0] - STAT_ROWS
    heads = rows // BLK
    lses = []
    for part in parts:
        stat = part[rows:, :].astype(jnp.float32)
        lses.append(stat[:heads] + stat[heads : 2 * heads] + stat[2 * heads : 3 * heads])
    top = functools.reduce(jnp.maximum, lses)
    weights = [jnp.exp2(lse - top) for lse in lses]
    share = 1.0 / functools.reduce(jnp.add, weights)
    weights = [w * share for w in weights]
    for h in range(heads):
        mixed = jnp.zeros((BLK, dh), jnp.float32)
        for part, w in zip(parts, weights):
            col = jnp.broadcast_to(w[h : h + 1, :], (BLK, BLK)).T
            mixed = mixed + part[h * BLK : (h + 1) * BLK, :].astype(jnp.float32) * col
        a_ref[:, h * dh : (h + 1) * dh] = mixed.astype(jnp.bfloat16)
    out_ref[...] = jnp.dot(a_ref[...], w_ref[0], preferred_element_type=jnp.float32).astype(jnp.bfloat16)


def project_kernel(a_ref, w_ref, *outs):
    for k, out in enumerate(outs):
        out[...] = jnp.dot(
            a_ref[...], w_ref[k + 1], preferred_element_type=jnp.float32
        ).astype(jnp.bfloat16)


def merge_project(parts, weight):
    ntp, depth, wide = weight.shape
    weight = pltpu.with_memory_space_constraint(weight, pltpu.VMEM)
    chunk = jax.ShapeDtypeStruct((BLK, wide), jnp.bfloat16)
    params = pltpu.CompilerParams(vmem_limit_bytes=16 * 2**20)
    mixed, out = pl.pallas_call(
        merge_kernel,
        out_shape=[jax.ShapeDtypeStruct((BLK, depth), jnp.bfloat16), chunk],
        in_specs=[VMEM()] * (len(parts) + 1),
        out_specs=[VMEM()] * 2,
        compiler_params=params,
        name="merge",
    )(*parts, weight)
    rest = pl.pallas_call(
        project_kernel,
        out_shape=[chunk] * (ntp - 1),
        in_specs=[VMEM()] * 2,
        out_specs=[VMEM()] * (ntp - 1),
        compiler_params=params,
        name="project",
    )(mixed, weight)
    return [out] + list(rest)


def decode_kernel(
    table_ref, meta_ref, parents_ref, q_ref, pool_ref, hand_ref, hist_ref, new_ref, out_ref, s_scr,
):
    rows, dh = q_ref.shape
    pages = pool_ref.shape[0]
    beams = hist_ref.shape[0]
    group = rows // (2 * beams)
    scale = dh ** (-0.5) * LOG2E
    length = meta_ref[0]
    n_hand = meta_ref[1]
    q = q_ref[...]
    row = lax.broadcasted_iota(jnp.int32, (rows, BLK), 0)
    lane = lax.broadcasted_iota(jnp.int32, (rows, BLK), 1)
    later = row >= rows // 2
    beam = (row // group) % beams
    parent = jnp.zeros_like(beam)
    for b in range(beams):
        parent = jnp.where(beam == b, parents_ref[b], parent)
    source = jnp.where(later, parent, beam)
    tiles = []
    for i in range(pages):
        tiles.append((functools.partial(lambda i: pool_ref[table_ref[i]], i), lane < length - i * BLK))
    for i in range(HANDED):
        slot = ((lane + i * BLK) // PIECE) % HANDED
        tiles.append((functools.partial(lambda i: hand_ref[i * BLK : (i + 1) * BLK], i), slot < n_hand))
    for b in range(beams):
        tiles.append((functools.partial(lambda b: hist_ref[b], b), source == b))
    fresh = ((lane < beams) & (source == lane)) | (
        (lane >= beams) & (lane < 2 * beams) & later & (beam == lane - beams)
    )
    tiles.append((lambda: new_ref[...], fresh))
    top = jnp.full((rows, BLK), FLOOR, jnp.float32)
    for t, (get, allowed) in enumerate(tiles):
        part = lax.dot_general(
            q, get()[:, :dh], (((1,), (1,)), ((), ())), preferred_element_type=jnp.float32
        ) * scale
        part = jnp.where(allowed, part, FLOOR)
        s_scr[t] = part
        top = jnp.maximum(top, part)
    top = jnp.max(top, axis=1, keepdims=True)
    total = jnp.zeros((rows, BLK), jnp.float32)
    acc = jnp.zeros((rows, dh), jnp.float32)
    for t, (get, _) in enumerate(tiles):
        weight = jnp.exp2(s_scr[t] - top)
        total = total + weight
        acc = acc + jnp.dot(
            weight.astype(jnp.bfloat16), get()[:, dh:], preferred_element_type=jnp.float32
        )
    out_ref[...] = (acc / jnp.sum(total, axis=1, keepdims=True)).astype(jnp.bfloat16)


def decode_attend(table, meta, parents, q, pool, hand, hist, new):
    rows, dh = q.shape
    tiles = pool.shape[0] + HANDED + hist.shape[0] + 1
    return pl.pallas_call(
        decode_kernel,
        out_shape=jax.ShapeDtypeStruct((rows, dh), jnp.bfloat16),
        in_specs=[SMEM(), SMEM(), SMEM(), VMEM(), VMEM(), VMEM(), VMEM(), VMEM()],
        out_specs=VMEM(),
        scratch_shapes=[pltpu.VMEM((tiles, rows, BLK), jnp.float32)],
        compiler_params=pltpu.CompilerParams(vmem_limit_bytes=16 * 2**20),
        name="decode_attend",
    )(table, meta, parents, q, pool, hand, hist, new)


def local(
    queries, span_kv, prior_kv, list_ids, out_weight, pool_kv, page_table, cache_lens,
    hist_kv, dec_q, dec_kv, parents, dest,
):
    nseq = lax.axis_size("seq")
    ntp = lax.axis_size("tp")
    me = lax.axis_index("seq")
    y, z, c = me // (NZ * NC), (me // NC) % NZ, me % NC
    span_len, group, dh = queries.shape[1:]
    width = 2 * dh
    kvb = prior_kv.shape[1] // BLK
    lists = list_ids[0]
    owner = lists // kvb

    mine = owner == me
    own_id = lists % kvb
    first = jnp.min(jnp.where(mine, own_id, kvb - 1), axis=1)
    last = jnp.max(jnp.where(mine, own_id, 0), axis=1)
    pick = jnp.stack([first, last], axis=1).reshape(NY, NZ, NC, SLOTS)

    offs = [2, 1, 3, 0]
    client = jnp.stack([seq_of(y, (z + off) % NZ, c) for off in offs])
    client_owner = jnp.take(owner, client, axis=0, mode="clip")
    srcs = jnp.arange(nseq).reshape(NY, NZ, NC)
    srcs = lax.dynamic_index_in_dim(srcs, z, 1, keepdims=False).reshape(PLANE)
    count = jnp.sum(client_owner[:, None, :] == srcs[None, :, None], axis=2)
    valid = (jnp.arange(SLOTS)[None, None, :] < count[:, :, None]).reshape(len(offs), -1)
    place = jnp.sum(
        valid[:, None, :] & (jnp.arange(SLOTS * PLANE)[None, :] < jnp.arange(SLOTS * PLANE)[:, None])[None],
        axis=2,
    )
    at = valid[:, None, :] & (place[:, None, :] == jnp.arange(SLOTS * PLANE)[None, :, None])
    order = jnp.sum(jnp.where(at, jnp.arange(SLOTS * PLANE)[None, None, :], 0), axis=2)
    tabs = jnp.concatenate([order, jnp.sum(count, axis=1)[:, None]], axis=1).astype(jnp.int32)

    blocks = prior_kv.reshape(kvb, BLK, width)
    span = span_kv.reshape(span_len, width)

    def picked(*offs):
        group = [lax.dynamic_index_in_dim(pick, (z + off) % NZ, 1, keepdims=False) for off in offs]
        return jnp.concatenate(group, axis=2).reshape(-1).astype(jnp.int32)

    def exchange(message):
        return lax.all_to_all(message, "seq", 0, 0, tiled=True, axis_index_groups=planes())

    def after(value, *others):
        return lax.optimization_barrier((value,) + others)[0]

    goal = dest[0]
    rank = jnp.sum(
        (goal[None, :] == goal[:, None]) & (jnp.arange(nseq)[None, :] < jnp.arange(nseq)[:, None]), axis=1
    )
    spots = jnp.arange(nseq)
    held = ((spots // NC) % NZ - z) % NZ * PLANE + spots // (NZ * NC) * NC + spots % NC
    sent = (goal[None, None, :] == srcs[:, None, None]) & (
        rank[None, None, :] == jnp.arange(HANDED)[None, :, None]
    )
    which = jnp.sum(jnp.where(sent, held[None, None, :], 0), axis=2).reshape(-1).astype(jnp.int32)
    n_hand = jnp.sum(goal == me)

    ask = queries[0].transpose(1, 0, 2).reshape(group * span_len, dh)
    here = lax.ppermute(span, "grp", [(0, 1), (1, 0)])
    there = {2: lax.ppermute(ask, "seq", z_shift(-2))}
    message = pack(blocks, picked(2), 1, "pieces", here.reshape(PLANE, PIECE, width))
    far = exchange(message)
    ask_late = after(ask, there[2])
    for off in (1, 3):
        there[off] = lax.ppermute(ask_late, "seq", z_shift(-off))
    pieces = far[:, SLOTS * BLK :, :]
    pieces = [pieces] + [lax.ppermute(pieces, "seq", z_shift(-off)) for off in (1, 2, 3)]
    message = pack(blocks, picked(1, 3), 2)
    near = exchange(after(message, far, there[2], which, n_hand, tabs))
    part = proxy_attend(tabs[0], there[2], far, 0)[0]
    backs = [lax.ppermute(after(part, *pieces), "seq", z_shift(2))]
    message = pack(blocks, picked(0), 1, "table", jnp.concatenate(pieces, axis=0), which)
    own = exchange(after(message, near, part, there[1], there[3]))
    for i, off in enumerate((1, 3)):
        part = proxy_attend(tabs[1 + i], there[off], near, i * SLOTS * BLK)[0]
        backs.append(lax.ppermute(part, "seq", z_shift(off)))
    handed = own[:, SLOTS * BLK :, :].reshape(HANDED * span_len, width)

    beams = hist_kv.shape[2]
    steps = dec_q.shape[1]
    new = dec_kv.reshape(steps * beams, width)
    new = jnp.concatenate([new, jnp.zeros((BLK - steps * beams, width), new.dtype)], axis=0)
    meta = jnp.stack([cache_lens[0, 0], n_hand]).astype(jnp.int32)
    decoded = decode_attend(
        page_table[0, 0], meta, parents[0, 0], dec_q.reshape(steps * beams * group, dh),
        pool_kv.reshape(-1, BLK, width), handed, hist_kv.reshape(beams, -1, width), new,
    )

    tp = lax.axis_index("tp")
    offsets = (2, 1, 3, 0)
    cols = jnp.stack([(tp + off) % ntp for off in offsets]).astype(jnp.int32)
    part, loaded = proxy_attend(tabs[3], ask, own, 0, span, cols, out_weight)
    outs = merge_project(backs + [part], loaded)
    summed = outs[-1].astype(jnp.float32)
    for off, out in zip(offsets[:-1], outs):
        got = lax.ppermute(out, "tp", [(i, (i + off) % ntp) for i in range(ntp)])
        summed = summed + got.astype(jnp.float32)
    return summed.astype(jnp.bfloat16)[None], decoded.reshape(dec_q.shape)


def solution(mesh):
    return jax.shard_map(
        local,
        mesh=mesh,
        in_specs=(
            P("grp", "seq", "tp", None),
            P("grp", "seq", "tp", None),
            P("grp", "seq", "tp", None),
            P("grp", None, None),
            P("tp", None),
            P("grp", "seq", None, None, "tp", None),
            P("grp", "seq", None),
            P("grp", "seq"),
            P("grp", "seq", None, None, "tp", None),
            P("grp", None, "seq", None, "tp", None),
            P("grp", None, "seq", None, "tp", None),
            P("grp", "seq", None),
            P("grp", None),
        ),
        out_specs=(P("grp", "seq", "tp"), P("grp", None, "seq", None, "tp", None)),
        check_vma=False,
    )
```

```python
import functools

import jax
import jax.numpy as jnp
from jax import lax
from jax.experimental import pallas as pl
from jax.experimental.pallas import tpu as pltpu
from jax.sharding import PartitionSpec as P

BLK = 128
SLOTS = 2
HANDED = 3
NY, NZ, NC = 4, 4, 2
PLANE = NY * NC
PIECE = BLK // PLANE
LOG2E = 1.4426950408889634
FLOOR = -1e30
STAT_ROWS = 32
ROWS = 512


def seq_of(y, z, c):
    return (y * NZ + z) * NC + c


def planes():
    return [[seq_of(y, z, c) for y in range(NY) for c in range(NC)] for z in range(NZ)]


def z_shift(by):
    return [
        (seq_of(y, z, c), seq_of(y, (z + by) % NZ, c))
        for y in range(NY)
        for z in range(NZ)
        for c in range(NC)
    ]


VMEM = functools.partial(pl.BlockSpec, memory_space=pltpu.VMEM)
SMEM = functools.partial(pl.BlockSpec, memory_space=pltpu.SMEM)
ANY = functools.partial(pl.BlockSpec, memory_space=pl.ANY)
HBM = functools.partial(pl.BlockSpec, memory_space=pltpu.HBM)


def pack_kernel(groups, extra, pick_ref, blocks, more, *rest):
    if extra == "table":
        which_ref, out, stage, sems_in, sems_out = rest
    else:
        out, stage, sems_in, sems_out = rest
    pairs = []

    def send(src, place):
        k = len(pairs)
        arrive = pltpu.make_async_copy(src, place(stage), sems_in.at[k])
        arrive.start()
        pairs.append((arrive, pltpu.make_async_copy(place(stage), place(out), sems_out.at[k])))

    each = groups * SLOTS
    rows = each * BLK
    for p in range(PLANE):
        for s in range(each):
            send(blocks.at[pick_ref[p * each + s]], lambda ref, p=p, s=s: ref.at[p, pl.ds(s * BLK, BLK), :])
    if extra == "pieces":
        for p in range(PLANE):
            send(more.at[p], lambda ref, p=p: ref.at[p, pl.ds(rows, PIECE), :])
    if extra == "table":
        for p in range(PLANE):
            for s in range(HANDED):
                send(
                    more.at[which_ref[p * HANDED + s]],
                    lambda ref, p=p, s=s: ref.at[p, pl.ds(rows + s * PIECE, PIECE), :],
                )
    for arrive, leave in pairs:
        arrive.wait()
        leave.start()
    for _, leave in pairs:
        leave.wait()


def pack(blocks, pick, groups, extra=None, more=None, which=None):
    width = blocks.shape[2]
    rows = groups * SLOTS * BLK + {None: 0, "pieces": PIECE, "table": HANDED * PIECE}[extra]
    count = groups * SLOTS * PLANE + {None: 0, "pieces": PLANE, "table": HANDED * PLANE}[extra]
    if more is None:
        more = jnp.zeros((8, 128), jnp.bfloat16)
    blocks = pltpu.with_memory_space_constraint(blocks, pltpu.HBM)
    args = [pick, blocks, more] + ([which] if extra == "table" else [])
    specs = [SMEM(), HBM(), ANY()] + ([SMEM()] if extra == "table" else [])
    return pl.pallas_call(
        functools.partial(pack_kernel, groups, extra),
        out_shape=pltpu.HBM((PLANE, rows, width), jnp.bfloat16),
        in_specs=specs,
        out_specs=HBM(),
        scratch_shapes=[
            pltpu.VMEM((PLANE, rows, width), jnp.bfloat16),
            pltpu.SemaphoreType.DMA((count,)),
            pltpu.SemaphoreType.DMA((count,)),
        ],
        compiler_params=pltpu.CompilerParams(vmem_limit_bytes=16 * 2**20),
        name="pack",
    )(*args)


def chunks(count, body):
    def four(k, _):
        body(4 * k, 4)
        return 0

    lax.fori_loop(0, count // 4, four, 0)

    @pl.when(count % 4 >= 2)
    def _():
        body(count // 4 * 4, 2)

    @pl.when(count % 2 == 1)
    def _():
        body(count - 1, 1)


def proxy_kernel(base, own, tab_ref, q_ref, kv_ref, *rest):
    if own:
        span_ref, col_ref, w_hbm, out_ref, w_ref, s_scr, m_scr, l_scr, acc_scr, k_scr, v_scr, sems = rest
        copies = []
        width = w_ref.shape[2]
        for i in range(w_ref.shape[0]):
            col = pl.multiple_of(col_ref[i] * width, width)
            copies.append(pltpu.make_async_copy(w_hbm.at[:, pl.ds(col, width)], w_ref.at[i], sems.at[i]))
            copies[-1].start()
    else:
        out_ref, s_scr, m_scr, l_scr, acc_scr, k_scr, v_scr = rest
    rows, dh = q_ref.shape
    scale = dh ** (-0.5) * LOG2E
    count = tab_ref[SLOTS * PLANE]
    m_scr[...] = jnp.full(m_scr.shape, FLOOR, jnp.float32)
    l_scr[...] = jnp.zeros(l_scr.shape, jnp.float32)
    acc_scr[...] = jnp.zeros(acc_scr.shape, jnp.float32)

    def score(k, many, mask=None):
        keys = k_scr[pl.ds(k, many)].reshape(many * BLK, dh)
        for r in range(0, rows, ROWS):
            part = lax.dot_general(
                q_ref[r : r + ROWS, :], keys, (((1,), (1,)), ((), ())), preferred_element_type=jnp.float32
            )
            if mask is not None:
                part = jnp.where(mask, part, FLOOR)
            top = m_scr[r : r + ROWS, :]
            for i in range(many):
                piece = part[:, i * BLK : (i + 1) * BLK]
                s_scr[k + i, r : r + ROWS, :] = piece
                top = jnp.maximum(top, piece)
            m_scr[r : r + ROWS, :] = top

    def first(k, many):
        for i in range(many):
            at = tab_ref[k + i]
            start = pl.multiple_of(base + (at % SLOTS) * BLK, BLK)
            block = kv_ref[at // SLOTS, pl.ds(start, BLK), :]
            k_scr[k + i] = block[:, :dh]
            v_scr[k + i] = block[:, dh:]
        score(k, many)

    chunks(count, first)
    if own:
        k_scr[count] = span_ref[:, :dh]
        v_scr[count] = span_ref[:, dh:]
        tok = lax.broadcasted_iota(jnp.int32, (ROWS, BLK), 0) % BLK
        key = lax.broadcasted_iota(jnp.int32, (ROWS, BLK), 1)
        score(count, 1, key <= tok)
        count = count + 1
    for r in range(0, rows, ROWS):
        top = jnp.max(m_scr[r : r + ROWS, :], axis=1, keepdims=True) * scale
        m_scr[r : r + ROWS, :] = jnp.broadcast_to(top, (ROWS, BLK))

    def mix(k, many):
        values = v_scr[pl.ds(k, many)].reshape(many * BLK, dh)
        for r in range(0, rows, ROWS):
            top = m_scr[r : r + ROWS, :]
            weights = [jnp.exp2(s_scr[k + i, r : r + ROWS, :] * scale - top) for i in range(many)]
            l_scr[r : r + ROWS, :] += functools.reduce(jnp.add, weights)
            weight = jnp.concatenate([w.astype(jnp.bfloat16) for w in weights], axis=1)
            acc_scr[r : r + ROWS, :] += jnp.dot(weight, values, preferred_element_type=jnp.float32)

    chunks(count, mix)
    heads = rows // BLK
    row = lax.broadcasted_iota(jnp.int32, (heads, BLK), 0)
    lse = jnp.zeros((heads, BLK), jnp.float32)
    for h in range(heads):
        sl = slice(h * BLK, (h + 1) * BLK)
        total = jnp.broadcast_to(jnp.sum(l_scr[sl, :], axis=1, keepdims=True), (BLK, BLK))
        some = total > 0.0
        safe = jnp.where(some, total, 1.0)
        out_ref[sl, :] = (acc_scr[sl, :] * (1.0 / safe)).astype(jnp.bfloat16)
        col = jnp.where(some, m_scr[sl, :] + jnp.log(safe) * LOG2E, FLOOR)
        lse = jnp.where(row == h, col.T[:heads, :], lse)
    one = lse.astype(jnp.bfloat16).astype(jnp.float32)
    two = (lse - one).astype(jnp.bfloat16).astype(jnp.float32)
    stat = jnp.concatenate([one, two, lse - one - two, jnp.zeros_like(lse)], axis=0)
    out_ref[rows:, :] = stat.astype(jnp.bfloat16)
    if own:
        for copy in copies:
            copy.wait()


def proxy_attend(tab, q, kv, base, span=None, cols=None, weight=None):
    rows, dh = q.shape
    own = span is not None
    blocks = SLOTS * PLANE + own
    kv = pltpu.with_memory_space_constraint(kv, pltpu.VMEM)
    out_shape = [jax.ShapeDtypeStruct((rows + STAT_ROWS, dh), jnp.bfloat16)]
    args, specs, sems = [tab, q, kv], [SMEM(), VMEM(), VMEM()], []
    if own:
        ntp = cols.shape[0]
        out_shape.append(pltpu.VMEM((ntp, weight.shape[0], weight.shape[1] // ntp), jnp.bfloat16))
        args += [span, cols, pltpu.with_memory_space_constraint(weight, pltpu.HBM)]
        specs += [VMEM(), SMEM(), HBM()]
        sems = [pltpu.SemaphoreType.DMA((ntp,))]
    return pl.pallas_call(
        functools.partial(proxy_kernel, base, own),
        out_shape=out_shape,
        in_specs=specs,
        out_specs=[VMEM()] * len(out_shape),
        scratch_shapes=[
            pltpu.VMEM((blocks, rows, BLK), jnp.float32),
            pltpu.VMEM((rows, BLK), jnp.float32),
            pltpu.VMEM((rows, BLK), jnp.float32),
            pltpu.VMEM((rows, dh), jnp.float32),
            pltpu.VMEM((blocks, BLK, dh), jnp.bfloat16),
            pltpu.VMEM((blocks, BLK, dh), jnp.bfloat16),
        ] + sems,
        compiler_params=pltpu.CompilerParams(vmem_limit_bytes=28 * 2**20),
        name="proxy_attend",
    )(*args)


def merge_kernel(part1, part2, part3, part4, w_ref, a_ref, out_ref):
    parts = (part1, part2, part3, part4)
    dh = part1.shape[1]
    rows = part1.shape[0] - STAT_ROWS
    heads = rows // BLK
    lses = []
    for part in parts:
        stat = part[rows:, :].astype(jnp.float32)
        lses.append(stat[:heads] + stat[heads : 2 * heads] + stat[2 * heads : 3 * heads])
    top = functools.reduce(jnp.maximum, lses)
    weights = [jnp.exp2(lse - top) for lse in lses]
    share = 1.0 / functools.reduce(jnp.add, weights)
    weights = [w * share for w in weights]
    for h in range(heads):
        mixed = jnp.zeros((BLK, dh), jnp.float32)
        for part, w in zip(parts, weights):
            col = jnp.broadcast_to(w[h : h + 1, :], (BLK, BLK)).T
            mixed = mixed + part[h * BLK : (h + 1) * BLK, :].astype(jnp.float32) * col
        a_ref[:, h * dh : (h + 1) * dh] = mixed.astype(jnp.bfloat16)
    out_ref[...] = jnp.dot(a_ref[...], w_ref[0], preferred_element_type=jnp.float32).astype(jnp.bfloat16)


def project_kernel(a_ref, w_ref, *outs):
    for k, out in enumerate(outs):
        out[...] = jnp.dot(
            a_ref[...], w_ref[k + 1], preferred_element_type=jnp.float32
        ).astype(jnp.bfloat16)


def merge_project(parts, weight):
    ntp, depth, wide = weight.shape
    weight = pltpu.with_memory_space_constraint(weight, pltpu.VMEM)
    chunk = jax.ShapeDtypeStruct((BLK, wide), jnp.bfloat16)
    params = pltpu.CompilerParams(vmem_limit_bytes=16 * 2**20)
    mixed, out = pl.pallas_call(
        merge_kernel,
        out_shape=[jax.ShapeDtypeStruct((BLK, depth), jnp.bfloat16), chunk],
        in_specs=[VMEM()] * (len(parts) + 1),
        out_specs=[VMEM()] * 2,
        compiler_params=params,
        name="merge",
    )(*parts, weight)
    rest = pl.pallas_call(
        project_kernel,
        out_shape=[chunk] * (ntp - 1),
        in_specs=[VMEM()] * 2,
        out_specs=[VMEM()] * (ntp - 1),
        compiler_params=params,
        name="project",
    )(mixed, weight)
    return [out] + list(rest)


def decode_kernel(
    table_ref, meta_ref, parents_ref, q_ref, pool_ref, hand_ref, hist_ref, new_ref, out_ref, s_scr,
):
    rows, dh = q_ref.shape
    pages = pool_ref.shape[0]
    beams = hist_ref.shape[0]
    group = rows // (2 * beams)
    scale = dh ** (-0.5) * LOG2E
    length = meta_ref[0]
    n_hand = meta_ref[1]
    q = q_ref[...]
    row = lax.broadcasted_iota(jnp.int32, (rows, BLK), 0)
    lane = lax.broadcasted_iota(jnp.int32, (rows, BLK), 1)
    later = row >= rows // 2
    beam = (row // group) % beams
    parent = jnp.zeros_like(beam)
    for b in range(beams):
        parent = jnp.where(beam == b, parents_ref[b], parent)
    source = jnp.where(later, parent, beam)
    tiles = []
    for i in range(pages):
        tiles.append((functools.partial(lambda i: pool_ref[table_ref[i]], i), lane < length - i * BLK))
    for i in range(HANDED):
        slot = ((lane + i * BLK) // PIECE) % HANDED
        tiles.append((functools.partial(lambda i: hand_ref[i * BLK : (i + 1) * BLK], i), slot < n_hand))
    for b in range(beams):
        tiles.append((functools.partial(lambda b: hist_ref[b], b), source == b))
    fresh = ((lane < beams) & (source == lane)) | (
        (lane >= beams) & (lane < 2 * beams) & later & (beam == lane - beams)
    )
    tiles.append((lambda: new_ref[...], fresh))
    top = jnp.full((rows, BLK), FLOOR, jnp.float32)
    for t, (get, allowed) in enumerate(tiles):
        part = lax.dot_general(
            q, get()[:, :dh], (((1,), (1,)), ((), ())), preferred_element_type=jnp.float32
        ) * scale
        part = jnp.where(allowed, part, FLOOR)
        s_scr[t] = part
        top = jnp.maximum(top, part)
    top = jnp.max(top, axis=1, keepdims=True)
    total = jnp.zeros((rows, BLK), jnp.float32)
    acc = jnp.zeros((rows, dh), jnp.float32)
    for t, (get, _) in enumerate(tiles):
        weight = jnp.exp2(s_scr[t] - top)
        total = total + weight
        acc = acc + jnp.dot(
            weight.astype(jnp.bfloat16), get()[:, dh:], preferred_element_type=jnp.float32
        )
    out_ref[...] = (acc / jnp.sum(total, axis=1, keepdims=True)).astype(jnp.bfloat16)


def decode_attend(table, meta, parents, q, pool, hand, hist, new):
    rows, dh = q.shape
    tiles = pool.shape[0] + HANDED + hist.shape[0] + 1
    return pl.pallas_call(
        decode_kernel,
        out_shape=jax.ShapeDtypeStruct((rows, dh), jnp.bfloat16),
        in_specs=[SMEM(), SMEM(), SMEM(), VMEM(), VMEM(), VMEM(), VMEM(), VMEM()],
        out_specs=VMEM(),
        scratch_shapes=[pltpu.VMEM((tiles, rows, BLK), jnp.float32)],
        compiler_params=pltpu.CompilerParams(vmem_limit_bytes=16 * 2**20),
        name="decode_attend",
    )(table, meta, parents, q, pool, hand, hist, new)


def local(
    queries, span_kv, prior_kv, list_ids, out_weight, pool_kv, page_table, cache_lens,
    hist_kv, dec_q, dec_kv, parents, dest,
):
    nseq = lax.axis_size("seq")
    ntp = lax.axis_size("tp")
    me = lax.axis_index("seq")
    y, z, c = me // (NZ * NC), (me // NC) % NZ, me % NC
    span_len, group, dh = queries.shape[1:]
    width = 2 * dh
    kvb = prior_kv.shape[1] // BLK
    lists = list_ids[0]
    owner = lists // kvb

    mine = owner == me
    own_id = lists % kvb
    first = jnp.min(jnp.where(mine, own_id, kvb - 1), axis=1)
    last = jnp.max(jnp.where(mine, own_id, 0), axis=1)
    pick = jnp.stack([first, last], axis=1).reshape(NY, NZ, NC, SLOTS)

    blocks = prior_kv.reshape(kvb, BLK, width)
    span = span_kv.reshape(span_len, width)

    def picked(*offs):
        group = [lax.dynamic_index_in_dim(pick, (z + off) % NZ, 1, keepdims=False) for off in offs]
        return jnp.concatenate(group, axis=2).reshape(-1).astype(jnp.int32)

    def exchange(message):
        return lax.all_to_all(message, "seq", 0, 0, tiled=True, axis_index_groups=planes())

    def after(value, *others):
        return lax.optimization_barrier((value,) + others)[0]

    here = lax.ppermute(span, "grp", [(0, 1), (1, 0)])
    message = pack(blocks, picked(2), 1, "pieces", here.reshape(PLANE, PIECE, width))
    asked, owner, goal, pick, message = lax.optimization_barrier(
        (queries[0], owner, dest[0], pick, message)
    )
    ask = asked.transpose(1, 0, 2).reshape(group * span_len, dh)
    there = {off: lax.ppermute(ask, "seq", z_shift(-off)) for off in (2, 1, 3)}

    offs = [2, 1, 3, 0]
    client = jnp.stack([seq_of(y, (z + off) % NZ, c) for off in offs])
    client_owner = jnp.take(owner, client, axis=0, mode="clip")
    srcs = jnp.arange(nseq).reshape(NY, NZ, NC)
    srcs = lax.dynamic_index_in_dim(srcs, z, 1, keepdims=False).reshape(PLANE)
    count = jnp.sum(client_owner[:, None, :] == srcs[None, :, None], axis=2)
    valid = (jnp.arange(SLOTS)[None, None, :] < count[:, :, None]).reshape(len(offs), -1)
    place = jnp.sum(
        valid[:, None, :] & (jnp.arange(SLOTS * PLANE)[None, :] < jnp.arange(SLOTS * PLANE)[:, None])[None],
        axis=2,
    )
    at = valid[:, None, :] & (place[:, None, :] == jnp.arange(SLOTS * PLANE)[None, :, None])
    order = jnp.sum(jnp.where(at, jnp.arange(SLOTS * PLANE)[None, None, :], 0), axis=2)
    tabs = jnp.concatenate([order, jnp.sum(count, axis=1)[:, None]], axis=1).astype(jnp.int32)

    rank = jnp.sum(
        (goal[None, :] == goal[:, None]) & (jnp.arange(nseq)[None, :] < jnp.arange(nseq)[:, None]), axis=1
    )
    spots = jnp.arange(nseq)
    held = ((spots // NC) % NZ - z) % NZ * PLANE + spots // (NZ * NC) * NC + spots % NC
    sent = (goal[None, None, :] == srcs[:, None, None]) & (
        rank[None, None, :] == jnp.arange(HANDED)[None, :, None]
    )
    which = jnp.sum(jnp.where(sent, held[None, None, :], 0), axis=2).reshape(-1).astype(jnp.int32)
    n_hand = jnp.sum(goal == me)

    far = exchange(message)
    message = pack(blocks, picked(1, 3), 2)
    near = exchange(after(message, far, there[2], which, n_hand, tabs))
    pieces = far[:, SLOTS * BLK :, :]
    pieces = [pieces] + [lax.ppermute(pieces, "seq", z_shift(-off)) for off in (1, 2, 3)]
    part = proxy_attend(tabs[0], there[2], far, 0)[0]
    backs = [lax.ppermute(after(part, *pieces), "seq", z_shift(2))]
    message = pack(blocks, picked(0), 1, "table", jnp.concatenate(pieces, axis=0), which)
    own = exchange(after(message, near, part, there[1], there[3]))
    for i, off in enumerate((1, 3)):
        part = proxy_attend(tabs[1 + i], there[off], near, i * SLOTS * BLK)[0]
        backs.append(lax.ppermute(part, "seq", z_shift(off)))
    handed = own[:, SLOTS * BLK :, :].reshape(HANDED * span_len, width)

    beams = hist_kv.shape[2]
    steps = dec_q.shape[1]
    new = dec_kv.reshape(steps * beams, width)
    new = jnp.concatenate([new, jnp.zeros((BLK - steps * beams, width), new.dtype)], axis=0)
    meta = jnp.stack([cache_lens[0, 0], n_hand]).astype(jnp.int32)
    decoded = decode_attend(
        page_table[0, 0], meta, parents[0, 0], dec_q.reshape(steps * beams * group, dh),
        pool_kv.reshape(-1, BLK, width), handed, hist_kv.reshape(beams, -1, width), new,
    )

    tp = lax.axis_index("tp")
    offsets = (2, 1, 3, 0)
    cols = jnp.stack([(tp + off) % ntp for off in offsets]).astype(jnp.int32)
    part, loaded = proxy_attend(tabs[3], ask, own, 0, span, cols, out_weight)
    outs = merge_project(backs + [part], loaded)
    summed = outs[-1].astype(jnp.float32)
    for off, out in zip(offsets[:-1], outs):
        got = lax.ppermute(out, "tp", [(i, (i + off) % ntp) for i in range(ntp)])
        summed = summed + got.astype(jnp.float32)
    return summed.astype(jnp.bfloat16)[None], decoded.reshape(dec_q.shape)


def solution(mesh):
    return jax.shard_map(
        local,
        mesh=mesh,
        in_specs=(
            P("grp", "seq", "tp", None),
            P("grp", "seq", "tp", None),
            P("grp", "seq", "tp", None),
            P("grp", None, None),
            P("tp", None),
            P("grp", "seq", None, None, "tp", None),
            P("grp", "seq", None),
            P("grp", "seq"),
            P("grp", "seq", None, None, "tp", None),
            P("grp", None, "seq", None, "tp", None),
            P("grp", None, "seq", None, "tp", None),
            P("grp", "seq", None),
            P("grp", None),
        ),
        out_specs=(P("grp", "seq", "tp"), P("grp", None, "seq", None, "tp", None)),
        check_vma=False,
    )
```
